512 devices in a mesh: row: 32 (over z_hi, x, core), col: 16 (over y, z_lo).
Axes of the slice: x: 4, y: 8, z: 8 (z_hi: 4, z_lo: 2; z = z_hi * 2 + z_lo), core: 2. Of those that a mesh axis runs over, the one named last changes fastest.
Arguments:
- feats: bfloat16 [65536, 256], P(('row', 'col')), may hold values from -6 to 6
- tiles: bfloat16 [32, 16, 96, 128, 128], P('row', 'col')
- tile_rows: int32 [32, 16, 96], P('row', 'col'), may hold values from 0 to 15, as said below
- tile_cols: int32 [32, 16, 96], P('row', 'col'), may hold values from 0 to 31
- tile_count: int32 [32, 16], P('row', 'col'), may hold values from 12 to 96
- w_self: bfloat16 [256, 256], replicated, may hold values from -0.375 to 0.375
- w_in: bfloat16 [256, 256], replicated, may hold values from -0.375 to 0.375
- w_out: bfloat16 [256, 256], replicated, may hold values from -0.375 to 0.375
- bias: float32 [256], replicated, may hold values from -3 to 3
Outputs:
- updated: bfloat16 [65536, 256], P(('row', 'col'))
The draws below stay inside these ranges and needn't reach their ends.
Inputs may be any that keep to these rules, and one draw needn't show every extreme that they name: `tile_rows`: within one device the live slots name distinct tile positions.
All inputs are finite; a program needn't handle non-finite values.
Results may differ from the reference program's by a relative error of at most 0.018.
Values may be sent and summed in bfloat16 or wider, within the bound.
No kernel may reach another device: no remote copies, remote signals or barrier semaphores. Data moves between devices by JAX's collectives and lax.ppermute only.
A program may use at most 64 MiB of HBM per device.

```python
import jax
import jax.numpy as jnp
from jax import lax

F = 256
NB = 128
TILE = 128
KT = 6
TPD = 96
NODES = 65536
N_ROW = 32
N_COL = 16


def tile_positions(key):
    positions = N_COL * NB // TILE * (N_ROW * NB // TILE)
    keys = jax.random.split(key, N_ROW * N_COL)
    chosen = jax.vmap(lambda single: jax.random.permutation(single, positions)[:TPD])(keys)
    return chosen.reshape(N_ROW, N_COL, TPD).astype(jnp.int32)


def draw_tile_rows(key, part):
    chosen = tile_positions(key)
    return (chosen // (N_ROW * NB // TILE)).astype(jnp.int32)


def draw_tile_cols(key, part):
    chosen = tile_positions(key)
    return (chosen % (N_ROW * NB // TILE)).astype(jnp.int32)


def draw_tile_count(key, part):
    key = jax.random.fold_in(key, 3)
    shifts = jax.random.randint(key, (N_ROW * N_COL,), 0, 4)
    counts = jnp.int32(TPD) // jnp.left_shift(jnp.int32(1), shifts.astype(jnp.int32))
    fullest = jax.random.randint(jax.random.fold_in(key, 5), (), 0, N_ROW * N_COL)
    counts = counts.at[fullest].set(TPD)
    return counts.reshape(N_ROW, N_COL).astype(jnp.int32)


def draw_tiles(key, part):
    key = jax.random.fold_in(key, 7)
    shape = (N_ROW, N_COL, TPD, TILE, TILE)
    fill = max(TILE // 8, 4) / TILE
    values = jax.random.normal(jax.random.fold_in(key, 1), shape, jnp.float32)
    present = jax.random.uniform(jax.random.fold_in(key, 2), shape, jnp.float32) < fill
    spread = (KT * N_COL * TILE * fill / 2.0) ** (-0.5)
    return jnp.where(present, values * spread, jnp.float32(0.0)).astype(jnp.bfloat16)


def block_scale(stream_key, extent, shards, least, high):
    factor_of = 1.0
    for position, blocks in shards:
        draws = jax.random.uniform(jax.random.fold_in(jax.random.fold_in(stream_key, 6), position), (blocks,), jnp.float32, least / len(shards), high / len(shards))
        factor_of = factor_of * jnp.repeat(jnp.exp(draws), extent[position] // blocks).reshape((-1,) + (1,) * (len(extent) - 1 - position))
    return factor_of


def bell_draw(stream_key, extent, scale, bound, cuts=(), held_as=jnp.bfloat16):
    entries = scale * jax.random.normal(stream_key, extent, jnp.float32)
    if cuts:
        entries = entries * block_scale(stream_key, extent, cuts, -0.22, 0.18)
    return jnp.clip(entries, -bound, bound).astype(held_as)


def setup_inputs(seed: int = 0) -> dict:
    key_of = jax.random.split(jax.random.key(seed), 10)
    feats = bell_draw(key_of[0], (NODES, F), 1.0, 6.0, ((0, 512),))
    tiles = draw_tiles(jax.random.fold_in(key_of[9], 71), 0)
    tile_rows = draw_tile_rows(jax.random.fold_in(key_of[9], 71), 0)
    tile_cols = draw_tile_cols(jax.random.fold_in(key_of[9], 71), 0)
    tile_count = draw_tile_count(jax.random.fold_in(key_of[9], 71), 0)
    w_self = bell_draw(key_of[5], (F, F), F ** -0.5, 0.375)
    w_in = bell_draw(key_of[6], (F, F), F ** -0.5, 0.375)
    w_out = bell_draw(key_of[7], (F, F), F ** -0.5, 0.375)
    bias = bell_draw(key_of[8], (F,), 0.5, 3.0, (), jnp.float32)
    return dict(feats=feats, tiles=tiles, tile_rows=tile_rows, tile_cols=tile_cols, tile_count=tile_count, w_self=w_self, w_in=w_in, w_out=w_out, bias=bias)


def reference(feats, tiles, tile_rows, tile_cols, tile_count, w_self, w_in, w_out, bias):
    rows_local = N_COL * NB // TILE
    cols_local = N_ROW * NB // TILE
    blocks = feats.reshape(N_ROW, N_COL, NB, F)
    flat_tiles = tiles.reshape(N_ROW * N_COL, TPD, TILE, TILE)
    flat_rows = tile_rows.reshape(N_ROW * N_COL, TPD)
    flat_cols = tile_cols.reshape(N_ROW * N_COL, TPD)
    flat_count = tile_count.reshape(N_ROW * N_COL)
    highest = lax.Precision.HIGHEST

    def device_terms(device, carry):
        in_sums, out_sums = carry
        row_id = device // N_COL
        col_id = device % N_COL
        column_panel = lax.dynamic_index_in_dim(blocks, col_id, 1, keepdims=False).reshape(cols_local, TILE, F)
        row_panel = lax.dynamic_index_in_dim(blocks, row_id, 0, keepdims=False).reshape(rows_local, TILE, F)
        own_tiles = lax.dynamic_index_in_dim(flat_tiles, device, 0, keepdims=False)
        own_rows = lax.dynamic_index_in_dim(flat_rows, device, 0, keepdims=False)
        own_cols = lax.dynamic_index_in_dim(flat_cols, device, 0, keepdims=False)
        own_count = lax.dynamic_index_in_dim(flat_count, device, 0, keepdims=False)
        live_slots = jnp.arange(TPD).astype(jnp.int32) < own_count
        masked = jnp.where(live_slots[:, None, None], own_tiles, jnp.zeros_like(own_tiles)).astype(jnp.float32)
        picked_in = column_panel[own_cols].astype(jnp.float32)
        products_in = jnp.einsum("sij,sjf->sif", masked, picked_in, precision=highest)
        select_rows = (jnp.arange(rows_local).astype(jnp.int32)[:, None] == own_rows[None, :]).astype(jnp.float32)
        term_in = jnp.einsum("rs,sif->rif", select_rows, products_in, precision=highest).reshape(rows_local * TILE, F)
        term_in = lax.optimization_barrier(term_in.astype(jnp.bfloat16)).astype(jnp.float32)
        picked_out = row_panel[own_rows].astype(jnp.float32)
        products_out = jnp.einsum("sji,sjf->sif", masked, picked_out, precision=highest)
        select_cols = (jnp.arange(cols_local).astype(jnp.int32)[:, None] == own_cols[None, :]).astype(jnp.float32)
        term_out = jnp.einsum("rs,sif->rif", select_cols, products_out, precision=highest).reshape(cols_local * TILE, F)
        term_out = lax.optimization_barrier(term_out.astype(jnp.bfloat16)).astype(jnp.float32)
        in_sums = in_sums.at[row_id].add(term_in)
        out_sums = out_sums.at[col_id].add(term_out)
        return in_sums, out_sums

    start_in = jnp.zeros((N_ROW, N_COL * NB, F), jnp.float32)
    start_out = jnp.zeros((N_COL, N_ROW * NB, F), jnp.float32)
    in_sums, out_sums = lax.fori_loop(0, N_ROW * N_COL, device_terms, (start_in, start_out))
    inward = in_sums.reshape(NODES, F).astype(jnp.bfloat16)
    outward = out_sums.reshape(N_COL, N_ROW, NB, F).transpose(1, 0, 2, 3).reshape(NODES, F).astype(jnp.bfloat16)
    total = jnp.dot(feats, w_self, preferred_element_type=jnp.float32)
    total = total + jnp.dot(inward, w_in, preferred_element_type=jnp.float32)
    total = total + jnp.dot(outward, w_out, preferred_element_type=jnp.float32)
    total = total + bias.astype(jnp.float32)[None, :]
    return jax.nn.relu(total).astype(jnp.bfloat16)
```

```python
import functools

import jax
import jax.numpy as jnp
from jax import lax
from jax.experimental import pallas as pl
from jax.experimental.pallas import tpu as pltpu
from jax.sharding import Mesh, PartitionSpec as P

ZH, X, CORE, Y, ZL = "zh", "x", "core", "y", "zl"
UNROLL = 8
VMEM_LIMIT = 40 * 2**20


def group_loop(count, body):
    lax.fori_loop(0, lax.div(count + (UNROLL - 1), UNROLL), lambda g, _: (body(g), 0)[1], 0)


def outward_kernel(scalars, rows, cols, tiles, panel, keep, send, acc):
    acc[...] = jnp.zeros_like(acc)
    count, core = scalars[0], scalars[1]

    def body(group):
        products = []
        for step in range(UNROLL):
            slot = group * UNROLL + step
            tile = jnp.where(slot < count, tiles[slot], jnp.zeros((), tiles.dtype))
            product = lax.dot_general(
                tile, panel[rows[slot]], (((0,), (0,)), ((), ())), preferred_element_type=jnp.float32
            )
            col = cols[slot]
            products.append(((((col & 1) ^ core) * 16) + (col >> 1), product))
        for place, product in products:
            acc[place] += product

    group_loop(count, body)
    keep[...] = acc[:16].astype(keep.dtype)
    send[...] = acc[16:].astype(send.dtype)


def inward_kernel(scalars, rows, cols, tiles, panel, out, acc):
    acc[...] = jnp.zeros_like(acc)
    count = scalars[0]

    def body(group):
        products = []
        for step in range(UNROLL):
            slot = group * UNROLL + step
            tile = jnp.where(slot < count, tiles[slot], jnp.zeros((), tiles.dtype))
            col = cols[slot]
            product = jnp.dot(
                tile, panel[(col & 1) * 16 + (col >> 1)], preferred_element_type=jnp.float32
            )
            products.append((rows[slot], product))
        for place, product in products:
            acc[place] += product

    group_loop(count, body)
    out[...] = acc[...].astype(out.dtype)


def final_kernel(feats, terms_in, terms_out, w_self, w_in, w_out, bias, out):
    def summed(terms):
        total = terms[0].astype(jnp.float32)
        for k in range(1, terms.shape[0]):
            total = total + terms[k].astype(jnp.float32)
        return total.astype(jnp.bfloat16)

    total = jnp.dot(feats[...], w_self[...], preferred_element_type=jnp.float32)
    total = total + jnp.dot(summed(terms_in), w_in[...], preferred_element_type=jnp.float32)
    total = total + jnp.dot(summed(terms_out), w_out[...], preferred_element_type=jnp.float32)
    out[...] = jnp.maximum(total + bias[...], 0.0).astype(out.dtype)


SMEM = pl.BlockSpec(memory_space=pltpu.SMEM)
VMEM = pl.BlockSpec(memory_space=pltpu.VMEM)


def spmm_call(kernel, outs, acc_tiles, scalars, rows, cols, tiles, panel):
    side, width = tiles.shape[-1], panel.shape[-1]
    return pl.pallas_call(
        kernel,
        out_shape=[jax.ShapeDtypeStruct((n, side, width), jnp.bfloat16) for n in outs],
        in_specs=[SMEM] * 3 + [VMEM] * 2,
        out_specs=[VMEM] * len(outs),
        scratch_shapes=[pltpu.VMEM((acc_tiles, side, width), jnp.float32)],
        compiler_params=pltpu.CompilerParams(vmem_limit_bytes=VMEM_LIMIT),
        cost_estimate=pl.CostEstimate(
            flops=2 * tiles.shape[0] * side * side * width,
            bytes_accessed=8 * 2**20,
            transcendentals=0,
        ),
    )(scalars, rows, cols, tiles, panel)


def exchange(parts, axes):
    return lax.all_to_all(parts, axes, 0, 0, tiled=True)


def per_device(feats, tiles, tile_rows, tile_cols, tile_count, w_self, w_in, w_out, bias):
    tiles, rows, cols = tiles[0, 0], tile_rows[0, 0], tile_cols[0, 0]
    core = lax.axis_index(CORE)
    scalars = jnp.stack([tile_count[0, 0], core.astype(jnp.int32)])
    side, width = feats.shape
    row_panel = lax.all_gather(lax.all_gather(feats, ZL), Y).reshape(16, side, width)
    col_panel = exchange(jnp.broadcast_to(feats[None], (16, side, width)), (ZH, X))
    col_panel = lax.all_gather(col_panel, CORE).reshape(32, side, width)
    keep, send = spmm_call(outward_kernel, (16, 16), 32, scalars, rows, cols, tiles, row_panel)
    got = lax.ppermute(send, CORE, [(0, 1), (1, 0)])
    (terms_in,) = spmm_call(inward_kernel, (16,), 16, scalars, rows, cols, tiles, col_panel)
    pair = (keep.astype(jnp.float32) + got.astype(jnp.float32)).astype(jnp.bfloat16)
    terms_out = exchange(pair, (ZH, X))
    terms_in = exchange(terms_in, (Y, ZL))
    return pl.pallas_call(
        final_kernel,
        out_shape=jax.ShapeDtypeStruct((side, width), jnp.bfloat16),
        in_specs=[VMEM] * 7,
        out_specs=VMEM,
        compiler_params=pltpu.CompilerParams(vmem_limit_bytes=VMEM_LIMIT),
    )(feats, terms_in, terms_out, w_self, w_in, w_out, bias[None, :])


def solution(mesh):
    split = Mesh(mesh.devices.reshape(4, 4, 2, 8, 2), (ZH, X, CORE, Y, ZL))
    row, col = (ZH, X, CORE), (Y, ZL)
    in_specs = (
        P(row + col, None),
        P(row, col, None, None, None),
        P(row, col, None),
        P(row, col, None),
        P(row, col),
        P(),
        P(),
        P(),
        P(),
    )
    return jax.shard_map(
        per_device, mesh=split, in_specs=in_specs, out_specs=P(row + col, None), check_vma=False
    )
```

```python
import functools

import jax
import jax.numpy as jnp
from jax import lax
from jax.experimental import pallas as pl
from jax.experimental.pallas import tpu as pltpu
from jax.sharding import Mesh, PartitionSpec as P

ZH, X, CORE, Y, ZL = "zh", "x", "core", "y", "zl"
UNROLL = 8
VMEM_LIMIT = 20 * 2**20
SMEM = pl.BlockSpec(memory_space=pltpu.SMEM)
VMEM = pl.BlockSpec(memory_space=pltpu.VMEM)
ANY = pl.BlockSpec(memory_space=pl.ANY)


def panel_place(block, own_zl):
    return (((block & 1) ^ own_zl) << 3) | (block >> 1)


def col_place(block, own_zl):
    return block ^ own_zl


def pair_place(block, core):
    return (((block & 1) ^ core) << 4) | (block >> 1)


def row_place(block, core, own_x):
    return (((block & 1) ^ core) << 4) | ((((block >> 1) & 3) ^ own_x) << 2) | (block >> 3)


def walk_slots(count, tiles, product, acc):
    acc[...] = jnp.zeros_like(acc)

    def body(group, _):
        done = []
        for step in range(UNROLL):
            slot = group * UNROLL + step
            tile = jnp.where(slot < count, tiles[slot], jnp.zeros((), tiles.dtype))
            done.append(product(slot, tile))
        for place, value in done:
            acc[place] += value
        return 0

    lax.fori_loop(0, lax.div(count + (UNROLL - 1), UNROLL), body, 0)


def fill(panel, parts):
    start = 0
    for part in parts:
        panel[start : start + part.shape[0]] = part[...]
        start += part.shape[0]


def outward_kernel(parts, scalars, rows, cols, tiles, *refs):
    keep, send, panel, acc = refs[-4:]
    fill(panel, refs[:parts])
    core, own_zl, own_x = scalars[1], scalars[2], scalars[3]

    def product(slot, tile):
        value = lax.dot_general(
            tile,
            panel[panel_place(rows[slot], own_zl)],
            (((0,), (0,)), ((), ())),
            preferred_element_type=jnp.float32,
        )
        return row_place(cols[slot], core, own_x), value

    walk_slots(scalars[0], tiles, product, acc)
    keep[...] = acc[:16].astype(keep.dtype)
    send[...] = acc[16:].astype(send.dtype)


def inward_kernel(parts, scalars, rows, cols, tiles, *refs):
    out, panel, acc = refs[-3:]
    fill(panel, refs[:parts])
    core, own_zl = scalars[1], scalars[2]

    def product(slot, tile):
        value = jnp.dot(
            tile, panel[pair_place(cols[slot], core)], preferred_element_type=jnp.float32
        )
        return col_place(rows[slot], own_zl), value

    walk_slots(scalars[0], tiles, product, acc)
    out[...] = acc[...].astype(out.dtype)


def add_kernel(terms, pieces, *refs):
    outs = refs[len(refs) - pieces :]
    size = outs[0].shape[0]
    for k, out in enumerate(outs):
        part = pl.ds(k * size, size)
        total = refs[0][part].astype(jnp.float32)
        for ref in refs[1:terms]:
            total = total + ref[part].astype(jnp.float32)
        out[...] = total.astype(out.dtype)


def final_kernel(feats, w_self, w_in, w_out, bias, terms_out, *refs):
    *terms_in, out = refs

    def product(terms, weight):
        total = terms[0].astype(jnp.float32)
        for term in terms[1:]:
            total = total + term.astype(jnp.float32)
        return jnp.dot(
            total.astype(jnp.bfloat16), weight[...], preferred_element_type=jnp.float32
        )

    total = jnp.dot(feats[...], w_self[...], preferred_element_type=jnp.float32)
    total = total + product([term[0] for term in terms_in], w_in)
    total = total + product([terms_out[k] for k in range(terms_out.shape[0])], w_out)
    out[...] = jnp.maximum(total + bias[...], 0.0).astype(out.dtype)


def copies_kernel(value, *refs):
    out = refs[-1]
    size = value.shape[0]
    for k in range(out.shape[0] // size):
        out[k * size : (k + 1) * size] = value[...]


def copies_call(value, count, after=()):
    return pl.pallas_call(
        copies_kernel,
        out_shape=jax.ShapeDtypeStruct((count * value.shape[0], *value.shape[1:]), value.dtype),
        in_specs=[VMEM] * (1 + len(after)),
        out_specs=VMEM,
        compiler_params=pltpu.CompilerParams(vmem_limit_bytes=VMEM_LIMIT),
        cost_estimate=pl.CostEstimate(
            flops=0, bytes_accessed=2 * (count + 1) * value.size, transcendentals=0
        ),
    )(value, *after)


def tie_kernel(*refs):
    pass


def tie_call(value, *after):
    return pl.pallas_call(
        tie_kernel,
        out_shape=jax.ShapeDtypeStruct(value.shape, value.dtype),
        in_specs=[ANY] * (1 + len(after)),
        out_specs=ANY,
        input_output_aliases={0: 0},
    )(value, *after)


def fold_kernel(parts, *outs):
    for k, out in enumerate(outs):
        total = parts[k].astype(jnp.float32)
        for start in range(len(outs), parts.shape[0], len(outs)):
            total = total + parts[start + k].astype(jnp.float32)
        out[...] = total[None].astype(out.dtype)


def fold_call(parts, pieces):
    shape = jax.ShapeDtypeStruct((1, *parts.shape[1:]), parts.dtype)
    return pl.pallas_call(
        fold_kernel,
        out_shape=[shape] * pieces,
        in_specs=[VMEM],
        out_specs=[VMEM] * pieces,
        compiler_params=pltpu.CompilerParams(vmem_limit_bytes=VMEM_LIMIT),
        cost_estimate=pl.CostEstimate(
            flops=parts.size, bytes_accessed=3 * parts.size, transcendentals=0
        ),
    )(parts)


def spmm_call(kernel, outs, out_tiles, panel_tiles, scalars, rows, cols, tiles, parts, after=()):
    side, width = tiles.shape[-1], parts[0].shape[-1]
    return pl.pallas_call(
        functools.partial(kernel, len(parts)),
        out_shape=[jax.ShapeDtypeStruct((out_tiles // outs, side, width), jnp.bfloat16)] * outs,
        in_specs=[SMEM] * 3 + [VMEM] * (1 + len(parts) + len(after)),
        out_specs=[VMEM] * outs,
        scratch_shapes=[
            pltpu.VMEM((panel_tiles, side, width), jnp.bfloat16),
            pltpu.VMEM((out_tiles, side, width), jnp.float32),
        ],
        compiler_params=pltpu.CompilerParams(vmem_limit_bytes=VMEM_LIMIT),
        cost_estimate=pl.CostEstimate(
            flops=2 * tiles.shape[0] * side * side * width,
            bytes_accessed=8 * 2**20,
            transcendentals=0,
        ),
    )(scalars, rows, cols, tiles, *parts, *after)


def add_call(terms, pieces, after=()):
    count, side, width = terms[0].shape
    size = terms[0].size
    return pl.pallas_call(
        functools.partial(add_kernel, len(terms), pieces),
        out_shape=[jax.ShapeDtypeStruct((count // pieces, side, width), jnp.bfloat16)] * pieces,
        in_specs=[VMEM] * (len(terms) + len(after)),
        out_specs=[VMEM] * pieces,
        compiler_params=pltpu.CompilerParams(vmem_limit_bytes=VMEM_LIMIT),
        cost_estimate=pl.CostEstimate(
            flops=size * len(terms), bytes_accessed=2 * size * (len(terms) + 1), transcendentals=0
        ),
    )(*terms, *after)


def exchange(parts, axis):
    return lax.all_to_all(parts, axis, 0, 0, tiled=True)


def swap(value, axis, bit):
    size = lax.axis_size(axis)
    return lax.ppermute(value, axis, [(i, i ^ bit) for i in range(size)])


def per_device(feats, tiles, tile_rows, tile_cols, tile_count, w_self, w_in, w_out, bias):
    tiles, rows, cols = tiles[0, 0], tile_rows[0, 0], tile_cols[0, 0]
    side, width = feats.shape
    scalars = jnp.stack(
        [tile_count[0, 0], lax.axis_index(CORE), lax.axis_index(ZL), lax.axis_index(X)]
    ).astype(jnp.int32)

    near_col = exchange(copies_call(feats[None], 16), (ZH, X))
    near_row = lax.all_gather(feats, Y)
    far_row = swap(near_row, ZL, 1)
    near_col = tie_call(near_col, near_row)
    far_col = swap(near_col, CORE, 1)

    (inward,) = spmm_call(
        inward_kernel, 1, 16, 32, scalars, rows, cols, tiles, (near_col, far_col)
    )
    keep_out, send_out = spmm_call(
        outward_kernel, 2, 32, 16, scalars, rows, cols, tiles, (near_row, far_row), (inward,)
    )
    inward = exchange(inward, Y)
    parts = add_call([keep_out, swap(send_out, CORE, 1)], 4)
    got = [swap(part, X, bit) for part, bit in zip(parts[1:], (1, 2, 3))]
    (outward,) = add_call([parts[0], *got], 1)
    terms_out = exchange(outward, ZH)
    keep, send = fold_call(inward, 2)
    terms_in = [keep, swap(send, ZL, 1)]
    return pl.pallas_call(
        final_kernel,
        out_shape=jax.ShapeDtypeStruct((side, width), jnp.bfloat16),
        in_specs=[VMEM] * 8,
        out_specs=VMEM,
        compiler_params=pltpu.CompilerParams(vmem_limit_bytes=VMEM_LIMIT),
    )(feats, w_self, w_in, w_out, bias[None, :], terms_out, *terms_in)


def solution(mesh):
    split = Mesh(mesh.devices.reshape(4, 4, 2, 8, 2), (ZH, X, CORE, Y, ZL))
    row, col = (ZH, X, CORE), (Y, ZL)
    in_specs = (
        P(row + col, None),
        P(row, col, None, None, None),
        P(row, col, None),
        P(row, col, None),
        P(row, col),
        P(),
        P(),
        P(),
        P(),
    )
    return jax.shard_map(
        per_device, mesh=split, in_specs=in_specs, out_specs=P(row + col, None), check_vma=False
    )
```

```python
import functools

import jax
import jax.numpy as jnp
from jax import lax
from jax.experimental import pallas as pl
from jax.experimental.pallas import tpu as pltpu
from jax.sharding import Mesh, PartitionSpec as P

ZH, X, CORE, YQ, YP, ZL = "zh", "x", "core", "yq", "yp", "zl"
UNROLL = 8
COST = 40000
VMEM_LIMIT = 20 * 2**20
SMEM = pl.BlockSpec(memory_space=pltpu.SMEM)
VMEM = pl.BlockSpec(memory_space=pltpu.VMEM)
ANY = pl.BlockSpec(memory_space=pl.ANY)


def panel_place(block, own):
    return (((block ^ own) & 2) << 2) | ((block >> 2) << 1) | (block & 1)


def col_place(block, own):
    d = block ^ own
    return ((d & 2) << 2) | ((d >> 2) << 1) | (d & 1)


def row_place(block, core):
    return (((block & 1) ^ core) << 4) | (block >> 1)


def walk_slots(count, tiles, product, acc):
    acc[...] = jnp.zeros_like(acc)

    def body(group, _):
        done = []
        for step in range(UNROLL):
            slot = group * UNROLL + step
            tile = jnp.where(slot < count, tiles[slot], jnp.zeros((), tiles.dtype))
            done.append(product(slot, tile))
        for place, value in done:
            acc[place] += value
        return 0

    lax.fori_loop(0, lax.div(count + (UNROLL - 1), UNROLL), body, 0)


def fill(panel, parts):
    start = 0
    for part in parts:
        panel[start : start + part.shape[0]] = part[...]
        start += part.shape[0]


def outward_kernel(parts, scalars, rows, cols, tiles, *refs):
    keep, send, token, panel, acc = refs[-5:]
    fill(panel, refs[:parts])
    core, own = scalars[1], scalars[2]

    def product(slot, tile):
        value = lax.dot_general(
            tile,
            panel[panel_place(rows[slot], own)],
            (((0,), (0,)), ((), ())),
            preferred_element_type=jnp.float32,
        )
        return row_place(cols[slot], core), value

    walk_slots(scalars[0], tiles, product, acc)
    keep[...] = acc[:16].astype(keep.dtype)
    send[...] = acc[16:].astype(send.dtype)
    token[...] = jnp.zeros_like(token)


def inward_kernel(parts, scalars, rows, cols, tiles, *refs):
    keep, send, token, panel, acc = refs[-5:]
    fill(panel, refs[:parts])
    core, own = scalars[1], scalars[2]

    def product(slot, tile):
        value = jnp.dot(
            tile, panel[row_place(cols[slot], core)], preferred_element_type=jnp.float32
        )
        return col_place(rows[slot], own), value

    walk_slots(scalars[0], tiles, product, acc)
    keep[...] = acc[:8].astype(keep.dtype)
    send[...] = acc[8:].astype(send.dtype)
    token[...] = jnp.zeros_like(token)


def add_kernel(terms, pieces, *refs):
    outs = refs[len(refs) - pieces :]
    size = outs[0].shape[0]
    for k, out in enumerate(outs):
        part = pl.ds(k * size, size)
        total = refs[0][part].astype(jnp.float32)
        for ref in refs[1:terms]:
            total = total + ref[part].astype(jnp.float32)
        out[...] = total.astype(out.dtype)


def final_kernel(feats, w_self, w_in, w_out, bias, terms_out, *refs):
    *terms_in, out = refs

    def product(terms, weight):
        total = terms[0].astype(jnp.float32)
        for term in terms[1:]:
            total = total + term.astype(jnp.float32)
        return jnp.dot(
            total.astype(jnp.bfloat16), weight[...], preferred_element_type=jnp.float32
        )

    total = jnp.dot(feats[...], w_self[...], preferred_element_type=jnp.float32)
    total = total + product([term[0] for term in terms_in], w_in)
    total = total + product([terms_out[k] for k in range(terms_out.shape[0])], w_out)
    out[...] = jnp.maximum(total + bias[...], 0.0).astype(out.dtype)


def copies_kernel(value, *refs):
    out = refs[-1]
    size = value.shape[0]
    for k in range(out.shape[0] // size):
        out[k * size : (k + 1) * size] = value[...]


def copies_call(value, count, after):
    return pl.pallas_call(
        copies_kernel,
        out_shape=jax.ShapeDtypeStruct((count * value.shape[0], *value.shape[1:]), value.dtype),
        in_specs=[VMEM, ANY],
        out_specs=VMEM,
        compiler_params=pltpu.CompilerParams(vmem_limit_bytes=VMEM_LIMIT),
        cost_estimate=pl.CostEstimate(
            flops=0, bytes_accessed=2 * (count + 1) * value.size, transcendentals=0
        ),
    )(value, after)


def spmm_call(kernel, out_tiles, panel_tiles, scalars, rows, cols, tiles, parts, after=()):
    side, width = tiles.shape[-1], parts[0].shape[-1]
    half = jax.ShapeDtypeStruct((out_tiles // 2, side, width), jnp.bfloat16)
    return pl.pallas_call(
        functools.partial(kernel, len(parts)),
        out_shape=[half, half, jax.ShapeDtypeStruct((8, 128), jnp.float32)],
        in_specs=[SMEM] * 3 + [VMEM] * (1 + len(parts) + len(after)),
        out_specs=[VMEM] * 3,
        scratch_shapes=[
            pltpu.VMEM((panel_tiles, side, width), jnp.bfloat16),
            pltpu.VMEM((out_tiles, side, width), jnp.float32),
        ],
        compiler_params=pltpu.CompilerParams(vmem_limit_bytes=VMEM_LIMIT),
        cost_estimate=pl.CostEstimate(
            flops=2 * tiles.shape[0] * side * side * width,
            bytes_accessed=8 * 2**20,
            transcendentals=0,
        ),
    )(scalars, rows, cols, tiles, *parts, *after)


def add_call(terms, pieces, after=(), cost=1):
    count, side, width = terms[0].shape
    size = terms[0].size
    return pl.pallas_call(
        functools.partial(add_kernel, len(terms), pieces),
        out_shape=[jax.ShapeDtypeStruct((count // pieces, side, width), jnp.bfloat16)] * pieces,
        in_specs=[VMEM] * (len(terms) + len(after)),
        out_specs=[VMEM] * pieces,
        compiler_params=pltpu.CompilerParams(vmem_limit_bytes=VMEM_LIMIT),
        cost_estimate=pl.CostEstimate(
            flops=cost * size * len(terms),
            bytes_accessed=2 * size * (len(terms) + 1),
            transcendentals=0,
        ),
    )(*terms, *after)


def exchange(parts, axis):
    return lax.all_to_all(parts, axis, 0, 0, tiled=True)


def swap(value, axis, bit):
    size = lax.axis_size(axis)
    return lax.ppermute(value, axis, [(i, i ^ bit) for i in range(size)])


def per_device(feats, tiles, tile_rows, tile_cols, tile_count, w_self, w_in, w_out, bias):
    tiles, rows, cols = tiles[0, 0], tile_rows[0, 0], tile_cols[0, 0]
    side, width = feats.shape
    own_col = lax.axis_index(YQ) * 4 + lax.axis_index(YP) * 2 + lax.axis_index(ZL)
    scalars = jnp.stack([tile_count[0, 0], lax.axis_index(CORE), own_col]).astype(jnp.int32)

    near_row = lax.all_gather(feats, ZL)
    near_col = exchange(copies_call(feats[None], 16, near_row), (ZH, X))
    far_col = swap(near_col, CORE, 1)
    near_row = lax.all_gather(near_row, YQ, axis=0, tiled=True)
    far_row = swap(near_row, YP, 1)

    keep_out, send_out, token = spmm_call(
        outward_kernel, 32, 16, scalars, rows, cols, tiles, (near_row, far_row)
    )
    got_out = swap(send_out, CORE, 1)
    keep, send, token = spmm_call(
        inward_kernel, 16, 32, scalars, rows, cols, tiles, (near_col, far_col), (token,)
    )
    (both,) = add_call([keep_out, got_out], 1, after=(token,))
    terms_out = exchange(both, (ZH, X))
    parts = add_call([keep, swap(send, YP, 1)], 4, cost=COST)
    got = [swap(part, YQ, bit) for part, bit in zip(parts[1:], (1, 2, 3))]
    keep, send = add_call([parts[0], *got], 2)
    terms_in = [keep, swap(send, ZL, 1)]
    return pl.pallas_call(
        final_kernel,
        out_shape=jax.ShapeDtypeStruct((side, width), jnp.bfloat16),
        in_specs=[VMEM] * 8,
        out_specs=VMEM,
        compiler_params=pltpu.CompilerParams(vmem_limit_bytes=VMEM_LIMIT),
    )(feats, w_self, w_in, w_out, bias[None, :], terms_out, *terms_in)


def solution(mesh):
    split = Mesh(mesh.devices.reshape(4, 4, 2, 4, 2, 2), (ZH, X, CORE, YQ, YP, ZL))
    row, col = (ZH, X, CORE), (YQ, YP, ZL)
    in_specs = (
        P(row + col, None),
        P(row, col, None, None, None),
        P(row, col, None),
        P(row, col, None),
        P(row, col),
        P(),
        P(),
        P(),
        P(),
    )
    return jax.shard_map(
        per_device, mesh=split, in_specs=in_specs, out_specs=P(row + col, None), check_vma=False
    )
```

```python
import functools

import jax
import jax.numpy as jnp
from jax import lax
from jax.experimental import pallas as pl
from jax.experimental.pallas import tpu as pltpu
from jax.sharding import Mesh, PartitionSpec as P

ZH, X, CORE, YQ, YP, ZL = "zh", "x", "core", "yq", "yp", "zl"
UNROLL = 32
COST = 20000
COST2 = 40000
TIE_COST = 10**11
VMEM_LIMIT = 20 * 2**20
SMEM = pl.BlockSpec(memory_space=pltpu.SMEM)
VMEM = pl.BlockSpec(memory_space=pltpu.VMEM)
ANY = pl.BlockSpec(memory_space=pl.ANY)


def panel_place(block, own):
    return (((block ^ own) & 2) << 2) | ((block >> 2) << 1) | (block & 1)


def col_place(block, own):
    d = block ^ own
    return ((d & 2) << 2) | ((d >> 2) << 1) | (d & 1)


def row_place(block, core):
    return (((block & 1) ^ core) << 4) | (block >> 1)


def term_place(block):
    return ((block & 1) << 4) | ((block & 6) << 1) | (block >> 3)


def walk_slots(count, tiles, product, acc):
    acc[...] = jnp.zeros_like(acc)

    def body(group, _):
        done = []
        for step in range(UNROLL):
            slot = group * UNROLL + step
            tile = jnp.where(slot < count, tiles[slot], jnp.zeros((), tiles.dtype))
            done.append(product(slot, tile))
        for place, value in done:
            acc[place] += value
        return 0

    lax.fori_loop(0, lax.div(count + (UNROLL - 1), UNROLL), body, 0)


def fill(panel, parts):
    start = 0
    for part in parts:
        panel[start : start + part.shape[0]] = part[...]
        start += part.shape[0]


def outward_kernel(parts, scalars, rows, cols, tiles, *refs):
    out, token, panel, acc = refs[-4:]
    fill(panel, refs[:parts])
    own = scalars[2]

    def product(slot, tile):
        value = lax.dot_general(
            tile,
            panel[panel_place(rows[slot], own)],
            (((0,), (0,)), ((), ())),
            preferred_element_type=jnp.float32,
        )
        return term_place(cols[slot]), value

    walk_slots(scalars[0], tiles, product, acc)
    out[...] = acc[...].astype(out.dtype)
    token[...] = jnp.zeros_like(token)


def inward_kernel(parts, scalars, rows, cols, tiles, *refs):
    keep, send, token, panel, acc = refs[-5:]
    fill(panel, refs[:parts])
    core, own = scalars[1], scalars[2]

    def product(slot, tile):
        value = jnp.dot(
            tile, panel[row_place(cols[slot], core)], preferred_element_type=jnp.float32
        )
        return col_place(rows[slot], own), value

    walk_slots(scalars[0], tiles, product, acc)
    keep[...] = acc[:8].astype(keep.dtype)
    send[...] = acc[8:].astype(send.dtype)
    token[...] = jnp.zeros_like(token)


def add_kernel(terms, pieces, *refs):
    outs = refs[len(refs) - pieces :]
    size = outs[0].shape[0]
    for k, out in enumerate(outs):
        part = pl.ds(k * size, size)
        total = refs[0][part].astype(jnp.float32)
        for ref in refs[1:terms]:
            total = total + ref[part].astype(jnp.float32)
        out[...] = total.astype(out.dtype)


def final_kernel(feats, w_self, w_in, w_out, bias, terms_out, *refs):
    *terms_in, out = refs

    def product(terms, weight):
        total = terms[0].astype(jnp.float32)
        for term in terms[1:]:
            total = total + term.astype(jnp.float32)
        return jnp.dot(
            total.astype(jnp.bfloat16), weight[...], preferred_element_type=jnp.float32
        )

    total = jnp.dot(feats[...], w_self[...], preferred_element_type=jnp.float32)
    total = total + product([term[0] for term in terms_in], w_in)
    total = total + product([terms_out[k] for k in range(terms_out.shape[0])], w_out)
    out[...] = jnp.maximum(total + bias[...], 0.0).astype(out.dtype)


def copies_kernel(value, *refs):
    out = refs[-1]
    size = value.shape[0]
    for k in range(out.shape[0] // size):
        out[k * size : (k + 1) * size] = value[...]


def copies_call(value, count, after):
    return pl.pallas_call(
        copies_kernel,
        out_shape=jax.ShapeDtypeStruct((count * value.shape[0], *value.shape[1:]), value.dtype),
        in_specs=[VMEM, ANY],
        out_specs=VMEM,
        compiler_params=pltpu.CompilerParams(vmem_limit_bytes=VMEM_LIMIT),
        cost_estimate=pl.CostEstimate(
            flops=0, bytes_accessed=2 * (count + 1) * value.size, transcendentals=0
        ),
    )(value, after)


def tie_kernel(value, *refs):
    refs[-1][...] = value[...]


def tie_call(value, after, cost=0):
    return pl.pallas_call(
        tie_kernel,
        out_shape=jax.ShapeDtypeStruct(value.shape, value.dtype),
        in_specs=[VMEM] + [ANY] * len(after),
        out_specs=VMEM,
        compiler_params=pltpu.CompilerParams(vmem_limit_bytes=VMEM_LIMIT),
        cost_estimate=pl.CostEstimate(
            flops=cost, bytes_accessed=4 * value.size, transcendentals=0
        ),
    )(value, *after)


def fold_kernel(parts, out):
    size = out.shape[0]
    total = parts[:size].astype(jnp.float32)
    for start in range(size, parts.shape[0], size):
        total = total + parts[start : start + size].astype(jnp.float32)
    out[...] = total.astype(out.dtype)


def fold_call(parts, count):
    return pl.pallas_call(
        fold_kernel,
        out_shape=jax.ShapeDtypeStruct((parts.shape[0] // count, *parts.shape[1:]), parts.dtype),
        in_specs=[VMEM],
        out_specs=VMEM,
        compiler_params=pltpu.CompilerParams(vmem_limit_bytes=VMEM_LIMIT),
        cost_estimate=pl.CostEstimate(
            flops=parts.size, bytes_accessed=3 * parts.size, transcendentals=0
        ),
    )(parts)


def spmm_call(kernel, out_tiles, panel_tiles, scalars, rows, cols, tiles, parts, after=(), outs=2):
    side, width = tiles.shape[-1], parts[0].shape[-1]
    part = jax.ShapeDtypeStruct((out_tiles // outs, side, width), jnp.bfloat16)
    return pl.pallas_call(
        functools.partial(kernel, len(parts)),
        out_shape=[part] * outs + [jax.ShapeDtypeStruct((8, 128), jnp.float32)],
        in_specs=[SMEM] * 3 + [VMEM] * (1 + len(parts) + len(after)),
        out_specs=[VMEM] * (outs + 1),
        scratch_shapes=[
            pltpu.VMEM((panel_tiles, side, width), jnp.bfloat16),
            pltpu.VMEM((out_tiles, side, width), jnp.float32),
        ],
        compiler_params=pltpu.CompilerParams(vmem_limit_bytes=VMEM_LIMIT),
        cost_estimate=pl.CostEstimate(
            flops=2 * tiles.shape[0] * side * side * width,
            bytes_accessed=8 * 2**20,
            transcendentals=0,
        ),
    )(scalars, rows, cols, tiles, *parts, *after)


def add_call(terms, pieces, after=(), cost=1):
    count, side, width = terms[0].shape
    size = terms[0].size
    return pl.pallas_call(
        functools.partial(add_kernel, len(terms), pieces),
        out_shape=[jax.ShapeDtypeStruct((count // pieces, side, width), jnp.bfloat16)] * pieces,
        in_specs=[VMEM] * (len(terms) + len(after)),
        out_specs=[VMEM] * pieces,
        compiler_params=pltpu.CompilerParams(vmem_limit_bytes=VMEM_LIMIT),
        cost_estimate=pl.CostEstimate(
            flops=cost * size * len(terms),
            bytes_accessed=2 * size * (len(terms) + 1),
            transcendentals=0,
        ),
    )(*terms, *after)


def exchange(parts, axis):
    return lax.all_to_all(parts, axis, 0, 0, tiled=True)


def swap(value, axis, bit):
    size = lax.axis_size(axis)
    return lax.ppermute(value, axis, [(i, i ^ bit) for i in range(size)])


def per_device(feats, tiles, tile_rows, tile_cols, tile_count, w_self, w_in, w_out, bias):
    tiles, rows, cols = tiles[0, 0], tile_rows[0, 0], tile_cols[0, 0]
    side, width = feats.shape
    own_col = lax.axis_index(YQ) * 4 + lax.axis_index(YP) * 2 + lax.axis_index(ZL)
    scalars = jnp.stack([tile_count[0, 0], lax.axis_index(CORE), own_col]).astype(jnp.int32)

    near_row = lax.all_gather(feats, ZL)
    near_col = exchange(copies_call(feats[None], 16, near_row), (ZH, X))
    near_row = lax.all_gather(near_row, YQ, axis=0, tiled=True)
    far_row = tie_call(swap(near_row, YP, 1), (), TIE_COST)
    near_col = tie_call(near_col, (near_row,))
    far_col = swap(near_col, CORE, 1)

    keep, send, token = spmm_call(
        inward_kernel,
        16,
        32,
        scalars,
        rows,
        cols,
        tiles,
        (near_col, far_col),
        (far_row,),
    )
    outward, token = spmm_call(
        outward_kernel, 32, 16, scalars, rows, cols, tiles, (near_row, far_row), (token,), 1
    )
    both = fold_call(exchange(outward, CORE), 2)
    terms_out = exchange(fold_call(exchange(both, X), 4), ZH)
    parts = add_call([keep, swap(send, YP, 1)], 4, cost=COST)
    got = [swap(part, YQ, bit) for part, bit in zip(parts[1:], (1, 2, 3))]
    keep, send = add_call([parts[0], *got], 2, cost=COST2)
    terms_in = [keep, swap(send, ZL, 1)]
    return pl.pallas_call(
        final_kernel,
        out_shape=jax.ShapeDtypeStruct((side, width), jnp.bfloat16),
        in_specs=[VMEM] * 8,
        out_specs=VMEM,
        compiler_params=pltpu.CompilerParams(vmem_limit_bytes=VMEM_LIMIT),
    )(feats, w_self, w_in, w_out, bias[None, :], terms_out, *terms_in)


def solution(mesh):
    split = Mesh(mesh.devices.reshape(4, 4, 2, 4, 2, 2), (ZH, X, CORE, YQ, YP, ZL))
    row, col = (ZH, X, CORE), (YQ, YP, ZL)
    in_specs = (
        P(row + col, None),
        P(row, col, None, None, None),
        P(row, col, None),
        P(row, col, None),
        P(row, col),
        P(),
        P(),
        P(),
        P(),
    )
    return jax.shard_map(
        per_device, mesh=split, in_specs=in_specs, out_specs=P(row + col, None), check_vma=False
    )
```

```python
import functools

import jax
import jax.numpy as jnp
from jax import lax
from jax.experimental import pallas as pl
from jax.experimental.pallas import tpu as pltpu
from jax.sharding import Mesh, PartitionSpec as P

ZH, X, CORE, YQ, YP, ZL = "zh", "x", "core", "yq", "yp", "zl"
UNROLL = 48
COST = 20000
COST2 = 40000
TIE_COST = 10**11
VMEM_LIMIT = 20 * 2**20
SMEM = pl.BlockSpec(memory_space=pltpu.SMEM)
VMEM = pl.BlockSpec(memory_space=pltpu.VMEM)
ANY = pl.BlockSpec(memory_space=pl.ANY)


def panel_place(block, own):
    return (((block ^ own) & 2) << 2) | ((block >> 2) << 1) | (block & 1)


def col_place(block, own):
    d = block ^ own
    return ((d & 2) << 2) | ((d >> 2) << 1) | (d & 1)


def row_place(block, core):
    return (((block & 1) ^ core) << 4) | (block >> 1)


def term_place(block):
    return ((block & 1) << 4) | ((block & 6) << 1) | (block >> 3)


def walk_slots(count, tiles, product, acc):
    acc[...] = jnp.zeros_like(acc)

    def body(group, _):
        done = []
        for step in range(UNROLL):
            slot = group * UNROLL + step
            tile = jnp.where(slot < count, tiles[slot], jnp.zeros((), tiles.dtype))
            done.append(product(slot, tile))
        for place, value in done:
            acc[place] += value
        return 0

    lax.fori_loop(0, lax.div(count + (UNROLL - 1), UNROLL), body, 0)


def fill(panel, parts):
    start = 0
    for part in parts:
        panel[start : start + part.shape[0]] = part[...]
        start += part.shape[0]


def outward_kernel(parts, scalars, rows, cols, tiles, *refs):
    out, token, panel, acc = refs[-4:]
    fill(panel, refs[:parts])
    own = scalars[2]

    def product(slot, tile):
        value = lax.dot_general(
            tile,
            panel[panel_place(rows[slot], own)],
            (((0,), (0,)), ((), ())),
            preferred_element_type=jnp.float32,
        )
        return term_place(cols[slot]), value

    walk_slots(scalars[0], tiles, product, acc)
    out[...] = acc[...].astype(out.dtype)
    token[...] = jnp.zeros_like(token)


def inward_kernel(parts, scalars, rows, cols, tiles, *refs):
    keep, send, token, panel, acc = refs[-5:]
    fill(panel, refs[:parts])
    core, own = scalars[1], scalars[2]

    def product(slot, tile):
        value = jnp.dot(
            tile, panel[row_place(cols[slot], core)], preferred_element_type=jnp.float32
        )
        return col_place(rows[slot], own), value

    walk_slots(scalars[0], tiles, product, acc)
    keep[...] = acc[:8].astype(keep.dtype)
    send[...] = acc[8:].astype(send.dtype)
    token[...] = jnp.zeros_like(token)


def add_kernel(terms, pieces, *refs):
    outs = refs[len(refs) - pieces :]
    size = outs[0].shape[0]
    for k, out in enumerate(outs):
        part = pl.ds(k * size, size)
        total = refs[0][part].astype(jnp.float32)
        for ref in refs[1:terms]:
            total = total + ref[part].astype(jnp.float32)
        out[...] = total.astype(out.dtype)


def final_kernel(feats, w_self, w_in, w_out, bias, terms_out, *refs):
    *terms_in, out = refs

    def product(terms, weight):
        total = terms[0].astype(jnp.float32)
        for term in terms[1:]:
            total = total + term.astype(jnp.float32)
        return jnp.dot(
            total.astype(jnp.bfloat16), weight[...], preferred_element_type=jnp.float32
        )

    total = jnp.dot(feats[...], w_self[...], preferred_element_type=jnp.float32)
    total = total + product([term[0] for term in terms_in], w_in)
    total = total + product([terms_out[k] for k in range(terms_out.shape[0])], w_out)
    out[...] = jnp.maximum(total + bias[...], 0.0).astype(out.dtype)


def copies_kernel(value, *refs):
    out = refs[-1]
    size = value.shape[0]
    for k in range(out.shape[0] // size):
        out[k * size : (k + 1) * size] = value[...]


def copies_call(value, count, after):
    return pl.pallas_call(
        copies_kernel,
        out_shape=jax.ShapeDtypeStruct((count * value.shape[0], *value.shape[1:]), value.dtype),
        in_specs=[VMEM, ANY],
        out_specs=VMEM,
        compiler_params=pltpu.CompilerParams(vmem_limit_bytes=VMEM_LIMIT),
        cost_estimate=pl.CostEstimate(
            flops=0, bytes_accessed=2 * (count + 1) * value.size, transcendentals=0
        ),
    )(value, after)


def tie_kernel(value, *refs):
    refs[-1][...] = value[...]


def tie_call(value, after, cost=0):
    return pl.pallas_call(
        tie_kernel,
        out_shape=jax.ShapeDtypeStruct(value.shape, value.dtype),
        in_specs=[VMEM] + [ANY] * len(after),
        out_specs=VMEM,
        compiler_params=pltpu.CompilerParams(vmem_limit_bytes=VMEM_LIMIT),
        cost_estimate=pl.CostEstimate(
            flops=cost, bytes_accessed=4 * value.size, transcendentals=0
        ),
    )(value, *after)


def fold_kernel(parts, out):
    size = out.shape[0]
    total = parts[:size].astype(jnp.float32)
    for start in range(size, parts.shape[0], size):
        total = total + parts[start : start + size].astype(jnp.float32)
    out[...] = total.astype(out.dtype)


def fold_call(parts, count):
    return pl.pallas_call(
        fold_kernel,
        out_shape=jax.ShapeDtypeStruct((parts.shape[0] // count, *parts.shape[1:]), parts.dtype),
        in_specs=[VMEM],
        out_specs=VMEM,
        compiler_params=pltpu.CompilerParams(vmem_limit_bytes=VMEM_LIMIT),
        cost_estimate=pl.CostEstimate(
            flops=parts.size, bytes_accessed=3 * parts.size, transcendentals=0
        ),
    )(parts)


def spmm_call(kernel, out_tiles, panel_tiles, scalars, rows, cols, tiles, parts, after=(), outs=2):
    side, width = tiles.shape[-1], parts[0].shape[-1]
    part = jax.ShapeDtypeStruct((out_tiles // outs, side, width), jnp.bfloat16)
    return pl.pallas_call(
        functools.partial(kernel, len(parts)),
        out_shape=[part] * outs + [jax.ShapeDtypeStruct((8, 128), jnp.float32)],
        in_specs=[SMEM] * 3 + [VMEM] * (1 + len(parts) + len(after)),
        out_specs=[VMEM] * (outs + 1),
        scratch_shapes=[
            pltpu.VMEM((panel_tiles, side, width), jnp.bfloat16),
            pltpu.VMEM((out_tiles, side, width), jnp.float32),
        ],
        compiler_params=pltpu.CompilerParams(vmem_limit_bytes=VMEM_LIMIT),
        cost_estimate=pl.CostEstimate(
            flops=2 * tiles.shape[0] * side * side * width,
            bytes_accessed=8 * 2**20,
            transcendentals=0,
        ),
    )(scalars, rows, cols, tiles, *parts, *after)


def add_call(terms, pieces, after=(), cost=1):
    count, side, width = terms[0].shape
    size = terms[0].size
    return pl.pallas_call(
        functools.partial(add_kernel, len(terms), pieces),
        out_shape=[jax.ShapeDtypeStruct((count // pieces, side, width), jnp.bfloat16)] * pieces,
        in_specs=[VMEM] * (len(terms) + len(after)),
        out_specs=[VMEM] * pieces,
        compiler_params=pltpu.CompilerParams(vmem_limit_bytes=VMEM_LIMIT),
        cost_estimate=pl.CostEstimate(
            flops=cost * size * len(terms),
            bytes_accessed=2 * size * (len(terms) + 1),
            transcendentals=0,
        ),
    )(*terms, *after)


def exchange(parts, axis):
    return lax.all_to_all(parts, axis, 0, 0, tiled=True)


def swap(value, axis, bit):
    size = lax.axis_size(axis)
    return lax.ppermute(value, axis, [(i, i ^ bit) for i in range(size)])


def per_device(feats, tiles, tile_rows, tile_cols, tile_count, w_self, w_in, w_out, bias):
    tiles, rows, cols = tiles[0, 0], tile_rows[0, 0], tile_cols[0, 0]
    side, width = feats.shape
    own_col = lax.axis_index(YQ) * 4 + lax.axis_index(YP) * 2 + lax.axis_index(ZL)
    scalars = jnp.stack([tile_count[0, 0], lax.axis_index(CORE), own_col]).astype(jnp.int32)

    near_row = lax.all_gather(feats, ZL)
    near_col = exchange(copies_call(feats[None], 16, near_row), (ZH, X))
    near_row = lax.all_gather(near_row, YQ, axis=0, tiled=True)
    far_row = tie_call(swap(near_row, YP, 1), (), TIE_COST)
    far_col = swap(near_col, CORE, 1)

    keep, send, token = spmm_call(
        inward_kernel,
        16,
        32,
        scalars,
        rows,
        cols,
        tiles,
        (near_col, far_col),
        (far_row,),
    )
    outward, token = spmm_call(
        outward_kernel, 32, 16, scalars, rows, cols, tiles, (near_row, far_row), (token,), 1
    )
    both = fold_call(exchange(outward, CORE), 2)
    terms_out = exchange(fold_call(exchange(both, X), 4), ZH)
    parts = add_call([keep, swap(send, YP, 1)], 4, cost=COST)
    got = [swap(part, YQ, bit) for part, bit in zip(parts[1:], (1, 2, 3))]
    keep, send = add_call([parts[0], *got], 2, cost=COST2)
    terms_in = [keep, swap(send, ZL, 1)]
    return pl.pallas_call(
        final_kernel,
        out_shape=jax.ShapeDtypeStruct((side, width), jnp.bfloat16),
        in_specs=[VMEM] * 8,
        out_specs=VMEM,
        compiler_params=pltpu.CompilerParams(vmem_limit_bytes=VMEM_LIMIT),
    )(feats, w_self, w_in, w_out, bias[None, :], terms_out, *terms_in)


def solution(mesh):
    split = Mesh(mesh.devices.reshape(4, 4, 2, 4, 2, 2), (ZH, X, CORE, YQ, YP, ZL))
    row, col = (ZH, X, CORE), (YQ, YP, ZL)
    in_specs = (
        P(row + col, None),
        P(row, col, None, None, None),
        P(row, col, None),
        P(row, col, None),
        P(row, col),
        P(),
        P(),
        P(),
        P(),
    )
    return jax.shard_map(
        per_device, mesh=split, in_specs=in_specs, out_specs=P(row + col, None), check_vma=False
    )
```

```python
import functools

import jax
import jax.numpy as jnp
from jax import lax
from jax.experimental import pallas as pl
from jax.experimental.pallas import tpu as pltpu
from jax.sharding import Mesh, PartitionSpec as P

ZH, X, CORE, YQ, YP, ZL = "zh", "x", "core", "yq", "yp", "zl"
UNROLL = 96
COST = 20000
COST2 = 40000
TIE_COST = 10**11
VMEM_LIMIT = 20 * 2**20
SMEM = pl.BlockSpec(memory_space=pltpu.SMEM)
VMEM = pl.BlockSpec(memory_space=pltpu.VMEM)
ANY = pl.BlockSpec(memory_space=pl.ANY)


def panel_place(block, own):
    return (((block ^ own) & 2) << 2) | ((block >> 2) << 1) | (block & 1)


def col_place(block, own):
    d = block ^ own
    return ((d & 2) << 2) | ((d >> 2) << 1) | (d & 1)


def row_place(block, core):
    return (((block & 1) ^ core) << 4) | (block >> 1)


def term_place(block):
    return ((block & 1) << 4) | ((block & 6) << 1) | (block >> 3)


def walk_slots(count, tiles, product, acc):
    acc[...] = jnp.zeros_like(acc)

    def body(group, _):
        done = []
        for step in range(UNROLL):
            slot = group * UNROLL + step
            tile = jnp.where(slot < count, tiles[slot], jnp.zeros((), tiles.dtype))
            done.append(product(slot, tile))
        for place, value in done:
            acc[place] += value
        return 0

    lax.fori_loop(0, lax.div(count + (UNROLL - 1), UNROLL), body, 0)


def fill(panel, parts):
    start = 0
    for part in parts:
        panel[start : start + part.shape[0]] = part[...]
        start += part.shape[0]


def outward_kernel(parts, scalars, rows, cols, tiles, *refs):
    out, token, panel, acc = refs[-4:]
    fill(panel, refs[:parts])
    own = scalars[2]

    def product(slot, tile):
        value = lax.dot_general(
            tile,
            panel[panel_place(rows[slot], own)],
            (((0,), (0,)), ((), ())),
            preferred_element_type=jnp.float32,
        )
        return term_place(cols[slot]), value

    walk_slots(scalars[0], tiles, product, acc)
    out[...] = acc[...].astype(out.dtype)
    token[...] = jnp.zeros_like(token)


def inward_kernel(parts, scalars, rows, cols, tiles, *refs):
    keep, send, token, panel, acc = refs[-5:]
    fill(panel, refs[:parts])
    core, own = scalars[1], scalars[2]

    def product(slot, tile):
        value = jnp.dot(
            tile, panel[row_place(cols[slot], core)], preferred_element_type=jnp.float32
        )
        return col_place(rows[slot], own), value

    walk_slots(scalars[0], tiles, product, acc)
    keep[...] = acc[:8].astype(keep.dtype)
    send[...] = acc[8:].astype(send.dtype)
    token[...] = jnp.zeros_like(token)


def add_kernel(terms, pieces, *refs):
    outs = refs[len(refs) - pieces :]
    size = outs[0].shape[0]
    for k, out in enumerate(outs):
        part = pl.ds(k * size, size)
        total = refs[0][part].astype(jnp.float32)
        for ref in refs[1:terms]:
            total = total + ref[part].astype(jnp.float32)
        out[...] = total.astype(out.dtype)


def final_kernel(feats, w_self, w_in, w_out, bias, terms_out, *refs):
    *terms_in, out = refs

    def product(terms, weight):
        total = terms[0].astype(jnp.float32)
        for term in terms[1:]:
            total = total + term.astype(jnp.float32)
        return jnp.dot(
            total.astype(jnp.bfloat16), weight[...], preferred_element_type=jnp.float32
        )

    total = jnp.dot(feats[...], w_self[...], preferred_element_type=jnp.float32)
    total = total + product([term[0] for term in terms_in], w_in)
    total = total + product([terms_out[k] for k in range(terms_out.shape[0])], w_out)
    out[...] = jnp.maximum(total + bias[...], 0.0).astype(out.dtype)


def copies_kernel(value, _, out, held, loaded, done):
    load = pltpu.make_async_copy(value, held, loaded)
    load.start()
    load.wait()
    copies = [pltpu.make_async_copy(held, out.at[k], done.at[k]) for k in range(out.shape[0])]
    for copy in copies:
        copy.start()
    for copy in copies:
        copy.wait()


def copies_call(value, count, after):
    return pl.pallas_call(
        copies_kernel,
        out_shape=jax.ShapeDtypeStruct((count, *value.shape), value.dtype),
        in_specs=[ANY, ANY],
        out_specs=ANY,
        scratch_shapes=[
            pltpu.VMEM(value.shape, value.dtype),
            pltpu.SemaphoreType.DMA,
            pltpu.SemaphoreType.DMA((count,)),
        ],
        cost_estimate=pl.CostEstimate(
            flops=0, bytes_accessed=2 * (count + 1) * value.size, transcendentals=0
        ),
    )(value, after)


def tie_kernel(value, *refs):
    refs[-1][...] = value[...]


def tie_call(value, after, cost=0):
    return pl.pallas_call(
        tie_kernel,
        out_shape=jax.ShapeDtypeStruct(value.shape, value.dtype),
        in_specs=[VMEM] + [ANY] * len(after),
        out_specs=VMEM,
        compiler_params=pltpu.CompilerParams(vmem_limit_bytes=VMEM_LIMIT),
        cost_estimate=pl.CostEstimate(
            flops=cost, bytes_accessed=4 * value.size, transcendentals=0
        ),
    )(value, *after)


def fold_kernel(parts, out):
    size = out.shape[0]
    total = parts[:size].astype(jnp.float32)
    for start in range(size, parts.shape[0], size):
        total = total + parts[start : start + size].astype(jnp.float32)
    out[...] = total.astype(out.dtype)


def fold_call(parts, count):
    return pl.pallas_call(
        fold_kernel,
        out_shape=jax.ShapeDtypeStruct((parts.shape[0] // count, *parts.shape[1:]), parts.dtype),
        in_specs=[VMEM],
        out_specs=VMEM,
        compiler_params=pltpu.CompilerParams(vmem_limit_bytes=VMEM_LIMIT),
        cost_estimate=pl.CostEstimate(
            flops=parts.size, bytes_accessed=3 * parts.size, transcendentals=0
        ),
    )(parts)


def spmm_call(kernel, out_tiles, panel_tiles, scalars, rows, cols, tiles, parts, after=(), outs=2):
    side, width = tiles.shape[-1], parts[0].shape[-1]
    part = jax.ShapeDtypeStruct((out_tiles // outs, side, width), jnp.bfloat16)
    return pl.pallas_call(
        functools.partial(kernel, len(parts)),
        out_shape=[part] * outs + [jax.ShapeDtypeStruct((8, 128), jnp.float32)],
        in_specs=[SMEM] * 3 + [VMEM] * (1 + len(parts) + len(after)),
        out_specs=[VMEM] * (outs + 1),
        scratch_shapes=[
            pltpu.VMEM((panel_tiles, side, width), jnp.bfloat16),
            pltpu.VMEM((out_tiles, side, width), jnp.float32),
        ],
        compiler_params=pltpu.CompilerParams(vmem_limit_bytes=VMEM_LIMIT),
        cost_estimate=pl.CostEstimate(
            flops=2 * tiles.shape[0] * side * side * width,
            bytes_accessed=8 * 2**20,
            transcendentals=0,
        ),
    )(scalars, rows, cols, tiles, *parts, *after)


def add_call(terms, pieces, after=(), cost=1):
    count, side, width = terms[0].shape
    size = terms[0].size
    return pl.pallas_call(
        functools.partial(add_kernel, len(terms), pieces),
        out_shape=[jax.ShapeDtypeStruct((count // pieces, side, width), jnp.bfloat16)] * pieces,
        in_specs=[VMEM] * (len(terms) + len(after)),
        out_specs=[VMEM] * pieces,
        compiler_params=pltpu.CompilerParams(vmem_limit_bytes=VMEM_LIMIT),
        cost_estimate=pl.CostEstimate(
            flops=cost * size * len(terms),
            bytes_accessed=2 * size * (len(terms) + 1),
            transcendentals=0,
        ),
    )(*terms, *after)


def exchange(parts, axis):
    return lax.all_to_all(parts, axis, 0, 0, tiled=True)


def swap(value, axis, bit):
    size = lax.axis_size(axis)
    return lax.ppermute(value, axis, [(i, i ^ bit) for i in range(size)])


def per_device(feats, tiles, tile_rows, tile_cols, tile_count, w_self, w_in, w_out, bias):
    tiles, rows, cols = tiles[0, 0], tile_rows[0, 0], tile_cols[0, 0]
    side, width = feats.shape
    own_col = lax.axis_index(YQ) * 4 + lax.axis_index(YP) * 2 + lax.axis_index(ZL)
    scalars = jnp.stack([tile_count[0, 0], lax.axis_index(CORE), own_col]).astype(jnp.int32)

    near_row = lax.all_gather(feats, ZL)
    near_col = exchange(copies_call(feats, 16, near_row), (ZH, X))
    near_row = lax.all_gather(near_row, YQ, axis=0, tiled=True)
    far_row = tie_call(swap(near_row, YP, 1), (), TIE_COST)
    far_col = swap(near_col, CORE, 1)

    keep, send, token = spmm_call(
        inward_kernel,
        16,
        32,
        scalars,
        rows,
        cols,
        tiles,
        (near_col, far_col),
        (far_row,),
    )
    outward, token = spmm_call(
        outward_kernel, 32, 16, scalars, rows, cols, tiles, (near_row, far_row), (token,), 1
    )
    both = fold_call(exchange(outward, CORE), 2)
    terms_out = exchange(fold_call(exchange(both, X), 4), ZH)
    parts = add_call([keep, swap(send, YP, 1)], 4, cost=COST)
    got = [swap(part, YQ, bit) for part, bit in zip(parts[1:], (1, 2, 3))]
    keep, send = add_call([parts[0], *got], 2, cost=COST2)
    terms_in = [keep, swap(send, ZL, 1)]
    return pl.pallas_call(
        final_kernel,
        out_shape=jax.ShapeDtypeStruct((side, width), jnp.bfloat16),
        in_specs=[VMEM] * 8,
        out_specs=VMEM,
        compiler_params=pltpu.CompilerParams(vmem_limit_bytes=VMEM_LIMIT),
    )(feats, w_self, w_in, w_out, bias[None, :], terms_out, *terms_in)


def solution(mesh):
    split = Mesh(mesh.devices.reshape(4, 4, 2, 4, 2, 2), (ZH, X, CORE, YQ, YP, ZL))
    row, col = (ZH, X, CORE), (YQ, YP, ZL)
    in_specs = (
        P(row + col, None),
        P(row, col, None, None, None),
        P(row, col, None),
        P(row, col, None),
        P(row, col),
        P(),
        P(),
        P(),
        P(),
    )
    return jax.shard_map(
        per_device, mesh=split, in_specs=in_specs, out_specs=P(row + col, None), check_vma=False
    )
```
